256 devices in a mesh: dp: 64 (over x, z, core), head: 4 (over y).
Axes of the slice: x: 4, y: 4, z: 8, core: 2. Of those that a mesh axis runs over, the one named last changes fastest.
Arguments:
- queries: bfloat16 [2, 16384, 8192], P(None, 'dp', 'head'), may hold values from -5 to 5
- keys: bfloat16 [2, 16384, 1024], P(None, 'dp', 'head'), may hold values from -5 to 5
- values: bfloat16 [2, 16384, 1024], P(None, 'dp', 'head'), may hold values from -5 to 5
- prefix_keys: bfloat16 [2, 128, 1024], P(None, None, 'head'), may hold values from -5 to 5
- prefix_values: bfloat16 [2, 128, 1024], P(None, None, 'head'), may hold values from -5 to 5
- dout: bfloat16 [2, 16384, 8192], P(None, 'dp', 'head'), may hold values from -6 to 6
- key_weight: bfloat16 [2, 8192, 1024], P(None, 'dp', 'head'), may hold values from -0.125 to 0.125
- value_weight: bfloat16 [2, 8192, 1024], P(None, 'dp', 'head'), may hold values from -0.125 to 0.125
Outputs:
- grad_queries: bfloat16 [2, 16384, 8192], P(None, 'dp', 'head')
- grad_input: bfloat16 [2, 16384, 8192], P(None, 'dp', 'head')
- grad_prefix_keys: float32 [2, 128, 1024], P(None, None, 'head')
- grad_prefix_values: float32 [2, 128, 1024], P(None, None, 'head')
The draws below stay inside these ranges and needn't reach their ends.
All inputs are finite; a program needn't handle non-finite values.
Results may differ from the reference program's by a relative error of at most 0.013.
Values may be sent and summed in bfloat16 or wider, within the bound.
No kernel may reach another device: no remote copies, remote signals or barrier semaphores. Data moves between devices by JAX's collectives and lax.ppermute only.
A program may use at most 128 MiB of HBM per device.

```python
import jax
import jax.numpy as jnp
from jax import lax

D = 8192
QH = 64
KVH = 8
HD = 128
PREFIX = 128
LEN = 256
LAYERS = 2
TOKENS = 16384
N_HEAD = 4


def draw_queries(key, part):
    own_key = jax.random.fold_in(key, 11)
    base = jnp.clip(jax.random.normal(own_key, (LAYERS, TOKENS, QH * HD), jnp.float32), -4.5, 4.5)
    return base.astype(jnp.bfloat16)


def draw_prefix_keys(key, part):
    own_key = jax.random.fold_in(key, 12)
    base = jnp.clip(jax.random.normal(own_key, (LAYERS, PREFIX, KVH * HD), jnp.float32), -4.5, 4.5)
    return base.astype(jnp.bfloat16)


def shard_levels(key, shape, cuts, least, largest):
    factor_of, own = 1.0, jax.random.fold_in(key, 6)
    for dim, blocks in cuts:
        draws = jnp.exp(jax.random.uniform(jax.random.fold_in(own, dim), (blocks,), jnp.float32, least / len(cuts), largest / len(cuts)))
        factor_of = factor_of * jnp.repeat(draws, shape[dim] // blocks).reshape([-1 if axis == dim else 1 for axis in range(len(shape))])
    return factor_of


def scatter_about(stream_key, dims, spread, bound, pieces=(), held_as=jnp.bfloat16):
    array = jax.random.normal(stream_key, dims, jnp.float32) * spread
    if len(pieces) > 0:
        array = shard_levels(stream_key, dims, pieces, -0.22, 0.18) * array
    return jnp.clip(array, min=-bound, max=bound).astype(held_as)


def setup_inputs(seed: int = 0) -> dict:
    arg_keys = jax.random.split(jax.random.key(seed), 9)
    return {
        "queries": draw_queries(jax.random.fold_in(arg_keys[8], 71), 0),
        "keys": scatter_about(arg_keys[1], (LAYERS, TOKENS, KVH * HD), 1.0, 5.0, ((1, 64), (2, 4))),
        "values": scatter_about(arg_keys[2], (LAYERS, TOKENS, KVH * HD), 1.0, 5.0, ((1, 64), (2, 4))),
        "prefix_keys": draw_prefix_keys(jax.random.fold_in(arg_keys[8], 71), 0),
        "prefix_values": scatter_about(arg_keys[4], (LAYERS, PREFIX, KVH * HD), 1.0, 5.0, ((2, 4),)),
        "dout": scatter_about(arg_keys[5], (LAYERS, TOKENS, QH * HD), 1.0, 6.0, ((1, 64), (2, 4))),
        "key_weight": scatter_about(arg_keys[6], (LAYERS, D, KVH * HD), (2 * KVH * HD) ** -0.5, 0.125, ((1, 64), (2, 4))),
        "value_weight": scatter_about(arg_keys[7], (LAYERS, D, KVH * HD), (2 * KVH * HD) ** -0.5, 0.125, ((1, 64), (2, 4))),
    }


def attend_back(queries, keys, values, pre_keys, pre_values, dout):
    seq_count, length, head_count, group_size, head_width = queries.shape
    prefix = pre_keys.shape[0]
    score_scale = head_width ** -0.5
    all_keys = jnp.concatenate([jnp.broadcast_to(pre_keys[None], (seq_count, prefix, head_count, head_width)), keys], axis=1)
    all_values = jnp.concatenate([jnp.broadcast_to(pre_values[None], (seq_count, prefix, head_count, head_width)), values], axis=1)
    position = jnp.arange(length)
    key_position = jnp.arange(prefix + length) - prefix
    visible = key_position[None, :] <= position[:, None]
    query_wide = queries.astype(jnp.float32)
    dout_wide = dout.astype(jnp.float32)
    keys_wide = all_keys.astype(jnp.float32)
    values_wide = all_values.astype(jnp.float32)
    scores = jnp.einsum("bskgh,bmkh->bkgsm", query_wide, keys_wide) * score_scale
    scores = jnp.where(visible, scores, -1e30)
    row_peak = jnp.max(scores, axis=-1, keepdims=True)
    exp_scores = jnp.exp(scores - row_peak)
    probs = exp_scores / jnp.sum(exp_scores, axis=-1, keepdims=True)
    probs_low = probs.astype(jnp.bfloat16)
    probs_back = probs_low.astype(jnp.float32)
    attended = jnp.einsum("bkgsm,bmkh->bskgh", probs_back, values_wide)
    row_delta = jnp.transpose(jnp.sum(dout_wide * attended, axis=-1), (0, 2, 3, 1))
    dprobs = jnp.einsum("bskgh,bmkh->bkgsm", dout_wide, values_wide)
    dscores = (probs * (dprobs - row_delta[..., None]) * score_scale).astype(jnp.bfloat16)
    dscores_wide = dscores.astype(jnp.float32)
    grad_query = jnp.einsum("bkgsm,bmkh->bskgh", dscores_wide, keys_wide).astype(jnp.bfloat16)
    key_terms = jnp.einsum("bkgsm,bskgh->bmkh", dscores_wide, query_wide)
    value_terms = jnp.einsum("bkgsm,bskgh->bmkh", probs_back, dout_wide)
    return (grad_query, key_terms[:, prefix:].astype(jnp.bfloat16), value_terms[:, prefix:].astype(jnp.bfloat16),
            jnp.sum(key_terms[:, :prefix], axis=0), jnp.sum(value_terms[:, :prefix], axis=0))


def reference(queries, keys, values, prefix_keys, prefix_values, dout, key_weight, value_weight):
    seq_total = TOKENS // LEN
    group_size = QH // KVH
    per_group = KVH // N_HEAD * HD
    query_list, input_list, key_list, value_list = [], [], [], []
    for layer_index in range(LAYERS):
        pre_keys = prefix_keys[layer_index].reshape(PREFIX, KVH, HD)
        pre_values = prefix_values[layer_index].reshape(PREFIX, KVH, HD)

        def one_sequence(items):
            query_one, key_one, value_one, dout_one = items
            return attend_back(query_one[None], key_one[None], value_one[None], pre_keys, pre_values, dout_one[None])

        results = lax.map(one_sequence, (
            queries[layer_index].reshape(seq_total, LEN, KVH, group_size, HD),
            keys[layer_index].reshape(seq_total, LEN, KVH, HD),
            values[layer_index].reshape(seq_total, LEN, KVH, HD),
            dout[layer_index].reshape(seq_total, LEN, KVH, group_size, HD)))
        grad_query, token_key, token_value, prefix_key, prefix_value = results
        query_list.append(grad_query.reshape(TOKENS, QH * HD))
        key_list.append(jnp.sum(prefix_key, axis=0).reshape(PREFIX, KVH * HD))
        value_list.append(jnp.sum(prefix_value, axis=0).reshape(PREFIX, KVH * HD))
        token_key = token_key.reshape(TOKENS, KVH * HD)
        token_value = token_value.reshape(TOKENS, KVH * HD)
        total = jnp.zeros((TOKENS, D), jnp.float32)
        for group_index in range(N_HEAD):
            low = group_index * per_group
            high = low + per_group
            flat = jnp.concatenate([token_key[:, low:high], token_value[:, low:high]], axis=1)
            weight_cols = jnp.concatenate([key_weight[layer_index][:, low:high], value_weight[layer_index][:, low:high]], axis=1)
            partial_value = jnp.dot(flat, weight_cols.T, preferred_element_type=jnp.float32)
            rounded = lax.optimization_barrier(partial_value.astype(jnp.bfloat16))
            total = total + rounded.astype(jnp.float32)
        input_list.append(total.astype(jnp.bfloat16))
    return jnp.stack(query_list), jnp.stack(input_list), jnp.stack(key_list), jnp.stack(value_list)
```

```python
import functools

import jax
import jax.numpy as jnp
from jax import lax
from jax.experimental import pallas as pl
from jax.experimental.pallas import tpu as pltpu
from jax.sharding import Mesh
from jax.sharding import PartitionSpec as P

QH = 64
KVH = 8
HD = 128
LEN = 256
PREFIX = 128
GROUP = QH // KVH
SCALE = HD ** (-0.5)
VMEM_LIMIT = 48 * 1024 * 1024

NT = (((1,), (1,)), ((), ()))
NN = (((1,), (0,)), ((), ()))
TN = (((0,), (0,)), ((), ()))


def dot(a, b, dims):
    return lax.dot_general(a, b, dims, preferred_element_type=jnp.float32)


def attend_kernel(q_ref, k_ref, v_ref, pk_ref, pv_ref, do_ref, gq_ref, flat_ref, gpk_ref, gpv_ref):
    head = pl.program_id(1)
    all_keys = jnp.concatenate([pk_ref[0], k_ref[0]], axis=0)
    all_values = jnp.concatenate([pv_ref[0], v_ref[0]], axis=0)
    rows = PREFIX + LEN
    key_position = lax.broadcasted_iota(jnp.int32, (rows, LEN), 0) - PREFIX
    token_position = lax.broadcasted_iota(jnp.int32, (rows, LEN), 1)
    visible = key_position <= token_position
    key_terms = jnp.zeros((rows, HD), jnp.float32)
    value_terms = jnp.zeros((rows, HD), jnp.float32)
    for h in range(GROUP):
        cols = slice(h * HD, (h + 1) * HD)
        q = q_ref[0, :, cols]
        do = do_ref[0, :, cols]
        scores = dot(all_keys, q, NT) * SCALE
        scores = jnp.where(visible, scores, -1e30)
        peak = jnp.max(scores, axis=0, keepdims=True)
        exp_scores = jnp.exp(scores - peak)
        probs = exp_scores * (1.0 / jnp.sum(exp_scores, axis=0, keepdims=True))
        probs_low = probs.astype(jnp.bfloat16)
        dprobs = dot(all_values, do, NT)
        row_delta = jnp.sum(probs_low.astype(jnp.float32) * dprobs, axis=0, keepdims=True)
        dscores = (probs * (dprobs - row_delta) * SCALE).astype(jnp.bfloat16)
        gq_ref[0, :, cols] = dot(dscores, all_keys, TN).astype(jnp.bfloat16)
        key_terms += dot(dscores, q, NN)
        value_terms += dot(probs_low, do, NN)
    start = pl.multiple_of(head * HD, HD)
    flat_ref[0, :, pl.ds(start, HD)] = key_terms[PREFIX:].astype(jnp.bfloat16)
    start = pl.multiple_of((head + 2) * HD, HD)
    flat_ref[0, :, pl.ds(start, HD)] = value_terms[PREFIX:].astype(jnp.bfloat16)
    gpk_ref[0] = key_terms[:PREFIX]
    gpv_ref[0] = value_terms[:PREFIX]


def attend_back(queries, keys, values, prefix_keys, prefix_values, dout):
    layers = queries.shape[0]
    heads = keys.shape[2] // HD
    wide = pl.BlockSpec((1, LEN, GROUP * HD), lambda l, k: (l, 0, k))
    own = pl.BlockSpec((1, LEN, HD), lambda l, k: (l, 0, k))
    pre = pl.BlockSpec((1, PREFIX, HD), lambda l, k: (l, 0, k))
    flat = pl.BlockSpec((1, LEN, 2 * heads * HD), lambda l, k: (l, 0, 0))
    return pl.pallas_call(
        attend_kernel,
        grid=(layers, heads),
        in_specs=[wide, own, own, pre, pre, wide],
        out_specs=[wide, flat, pre, pre],
        out_shape=[
            jax.ShapeDtypeStruct(queries.shape, jnp.bfloat16),
            jax.ShapeDtypeStruct((layers, LEN, 2 * heads * HD), jnp.bfloat16),
            jax.ShapeDtypeStruct((layers, PREFIX, heads * HD), jnp.float32),
            jax.ShapeDtypeStruct((layers, PREFIX, heads * HD), jnp.float32),
        ],
        compiler_params=pltpu.CompilerParams(vmem_limit_bytes=VMEM_LIMIT),
        cost_estimate=pl.CostEstimate(
            flops=5 * 2 * layers * heads * GROUP * LEN * (PREFIX + LEN) * HD,
            bytes_accessed=8 * 1024 * 1024,
            transcendentals=layers * heads * GROUP * LEN * (PREFIX + LEN),
        ),
    )(queries, keys, values, prefix_keys, prefix_values, dout)


def project_kernel(y_ref, *refs):
    (f0, f1, f2, f3, g0, g1, g2, g3, w0, w1, w2, w3, mine_ref, other_ref) = refs
    total = [None, None]
    for side, group in enumerate(((f0, f1, f2, f3), (g0, g1, g2, g3))):
        acc = None
        for f, w in zip(group, (w0, w1, w2, w3)):
            rows = w[0, :, 0].reshape(-1, w.shape[-1])
            term = dot(f[0], rows, NT)
            acc = term if acc is None else acc + term
        total[side] = acc.astype(jnp.bfloat16)
    mine_ref[0] = total[0]
    other_ref[0] = total[1]


def project(own, other, weights, y):
    layers, tokens, width = own[0].shape
    y_count, z_count, _, rows, _ = weights.shape
    step = 2
    flat_spec = pl.BlockSpec((1, tokens, width), lambda l, n, y_ref: (l, 0, 0))

    def weight_spec(shift):
        return pl.BlockSpec(
            (1, step, 1, rows, width),
            lambda l, n, y_ref: (lax.rem(y_ref[0] + (y_count - shift), y_count), n, l, 0, 0),
        )

    out_spec = pl.BlockSpec((1, tokens, step * rows), lambda l, n, y_ref: (l, 0, n))
    out_type = jax.ShapeDtypeStruct((layers, tokens, z_count * rows), jnp.bfloat16)
    return pl.pallas_call(
        project_kernel,
        grid_spec=pltpu.PrefetchScalarGridSpec(
            num_scalar_prefetch=1,
            grid=(layers, z_count // step),
            in_specs=[flat_spec] * 8 + [weight_spec(s) for s in range(4)],
            out_specs=[out_spec, out_spec],
        ),
        out_shape=[out_type, out_type],
        compiler_params=pltpu.CompilerParams(vmem_limit_bytes=VMEM_LIMIT),
        cost_estimate=pl.CostEstimate(
            flops=2 * layers * 2 * tokens * z_count * rows * y_count * width,
            bytes_accessed=14 * 1024 * 1024,
            transcendentals=0,
        ),
    )(y, *own, *other, weights, weights, weights, weights)


def weave_kernel(core_ref, mine_ref, theirs_ref, out_ref):
    mine = mine_ref[0]
    theirs = theirs_ref[0]
    first = core_ref[0] == 0
    rows = 128
    for j in range(mine.shape[1] // rows):
        cols = slice(j * rows, (j + 1) * rows)
        a = mine[:, cols]
        b = theirs[:, cols]
        out_ref[0, :, 2 * j * rows : (2 * j + 1) * rows] = jnp.where(first, a, b)
        out_ref[0, :, (2 * j + 1) * rows : (2 * j + 2) * rows] = jnp.where(first, b, a)


def weave(mine, theirs, core):
    layers, tokens, width = mine.shape
    step = 512
    part = pl.BlockSpec((1, tokens, step), lambda l, n, c: (l, 0, n))
    return pl.pallas_call(
        weave_kernel,
        grid_spec=pltpu.PrefetchScalarGridSpec(
            num_scalar_prefetch=1,
            grid=(layers, width // step),
            in_specs=[part, part],
            out_specs=pl.BlockSpec((1, tokens, 2 * step), lambda l, n, c: (l, 0, n)),
        ),
        out_shape=jax.ShapeDtypeStruct((layers, tokens, 2 * width), jnp.bfloat16),
        compiler_params=pltpu.CompilerParams(vmem_limit_bytes=VMEM_LIMIT),
    )(core, mine, theirs)


def ring(count, shift):
    return [(i, (i + shift) % count) for i in range(count)]


def swap_cores(a):
    return lax.ppermute(a, "core", [(0, 1), (1, 0)])


def sum_prefix(gpk, gpv, core, replicas):
    layers, rows, width = gpk.shape
    keep = jnp.where(core == 0, gpk, gpv)
    send = jnp.where(core == 0, gpv, gpk)
    half = (keep + swap_cores(send)).reshape(layers * rows, width)
    pieces = lax.all_to_all(half, ("x", "z"), 0, 0, tiled=True)
    piece = jnp.sum(pieces.reshape(replicas, -1, width), axis=0)
    spread = jnp.broadcast_to(piece[None], (replicas,) + piece.shape).reshape(-1, width)
    whole = lax.all_to_all(spread, ("x", "z"), 0, 0, tiled=True).reshape(layers, rows, width)
    theirs = swap_cores(whole)
    return jnp.where(core == 0, whole, theirs), jnp.where(core == 0, theirs, whole)


def shards(queries, keys, values, prefix_keys, prefix_values, dout, key_weight, value_weight):
    y = lax.axis_index("y").reshape(1).astype(jnp.int32)
    core = lax.axis_index("core")
    stacked = jnp.concatenate([key_weight, value_weight], axis=2)
    turned = lax.ppermute(
        stacked, ("x", "y"), [(i * 4 + j, j * 4 + i) for i in range(4) for j in range(4)]
    )
    weights = lax.all_gather(turned, ("x", "z"), axis=0)
    weights = weights.reshape((4, 8) + turned.shape)
    grad_queries, flat, gpk, gpv = attend_back(
        queries, keys, values, prefix_keys, prefix_values, dout
    )
    own = [flat] + [lax.ppermute(flat, "y", ring(4, s)) for s in (1, 2, 3)]
    other = [swap_cores(a) for a in own]
    grad_prefix_keys, grad_prefix_values = sum_prefix(gpk, gpv, core, 32)
    mine, give = project(own, other, weights, y)
    theirs = swap_cores(give)
    grad_input = weave(mine, theirs, core.reshape(1).astype(jnp.int32))
    return grad_queries, grad_input, grad_prefix_keys, grad_prefix_values


def solution(mesh):
    mesh = Mesh(mesh.devices.reshape(4, 8, 2, 4), ("x", "z", "core", "y"))
    dp = ("x", "z", "core")
    split = P(None, dp, "y")
    shared = P(None, None, "y")
    in_specs = (split, split, split, shared, shared, split, split, split)
    out_specs = (split, split, shared, shared)
    return jax.shard_map(shards, mesh=mesh, in_specs=in_specs, out_specs=out_specs, check_vma=False)
```

```python
import functools
import math

import jax
import jax.numpy as jnp
from jax import lax
from jax.experimental import pallas as pl
from jax.experimental.pallas import tpu as pltpu
from jax.sharding import Mesh
from jax.sharding import PartitionSpec as P

QH = 64
KVH = 8
HD = 128
LEN = 256
PREFIX = 128
GROUP = QH // KVH
SCALE = HD ** (-0.5)
VMEM_LIMIT = 60 * 1024 * 1024
EXP2 = SCALE * math.log2(math.e)
COST = pl.CostEstimate(flops=2 * 10**9, bytes_accessed=16 * 10**6, transcendentals=0)
BRIEF = pl.CostEstimate(flops=1, bytes_accessed=1, transcendentals=0)

NT = (((1,), (1,)), ((), ()))
NN = (((1,), (0,)), ((), ()))
TN = (((0,), (0,)), ((), ()))


def dot(a, b, dims):
    return lax.dot_general(a, b, dims, preferred_element_type=jnp.float32)


def attend_kernel(q_ref, k_ref, v_ref, pk_ref, pv_ref, do_ref, gq_ref, flat_ref, terms_ref):
    half = LEN // 2
    keys = jnp.concatenate([pk_ref[0], k_ref[0]], axis=0)
    values = jnp.concatenate([pv_ref[0], v_ref[0]], axis=0)
    key_row = lax.broadcasted_iota(jnp.int32, (half, 2 * half), 0)
    token = lax.rem(lax.broadcasted_iota(jnp.int32, (half, 2 * half), 1), half)
    visible = key_row <= token
    key_terms = [0.0, 0.0]
    value_terms = [0.0, 0.0]
    for pair in range(GROUP // 2):
        for part in range(2):
            rows = PREFIX + (part + 1) * half
            tokens = slice(part * half, (part + 1) * half)
            columns = [slice((2 * pair + i) * HD, (2 * pair + i + 1) * HD) for i in range(2)]
            q = jnp.concatenate([q_ref[0, tokens, c] for c in columns], axis=0)
            do = jnp.concatenate([do_ref[0, tokens, c] for c in columns], axis=0)
            scores = dot(keys[:rows], q, NT)
            last = jnp.where(visible, scores[rows - half :], -1e30)
            scores = jnp.concatenate([scores[: rows - half], last], axis=0)
            peak = jnp.max(scores, axis=0, keepdims=True)
            exp_scores = jnp.exp2((scores - peak) * EXP2)
            probs = exp_scores * (1.0 / jnp.sum(exp_scores, axis=0, keepdims=True))
            dprobs = dot(values[:rows], do, NT)
            row_delta = jnp.sum(probs * dprobs, axis=0, keepdims=True)
            dscores = (probs * (dprobs - row_delta)).astype(jnp.bfloat16)
            gq = (dot(dscores, keys[:rows], TN) * SCALE).astype(jnp.bfloat16)
            for i, c in enumerate(columns):
                gq_ref[0, tokens, c] = gq[i * half : (i + 1) * half]
            key_terms[part] += dot(dscores, q, NN)
            value_terms[part] += dot(probs.astype(jnp.bfloat16), do, NN)
    split = PREFIX + half
    for i, (terms, scale) in enumerate(((key_terms, SCALE), (value_terms, 1.0))):
        low = (terms[0] + terms[1][:split]) * scale
        high = terms[1][split:] * scale
        flat_ref[0, :half, i * HD : (i + 1) * HD] = low[PREFIX:].astype(jnp.bfloat16)
        flat_ref[0, half:, i * HD : (i + 1) * HD] = high.astype(jnp.bfloat16)
        terms_ref[i, 0] = low[:PREFIX]


def attend_back(queries, keys, values, prefix_keys, prefix_values, dout):
    layers, _, width = keys.shape
    heads = width // HD
    wide = pl.BlockSpec((1, LEN, GROUP * HD), lambda l, h: (l, 0, h))
    own = pl.BlockSpec((1, LEN, HD), lambda l, h: (l, 0, h))
    pre = pl.BlockSpec((1, PREFIX, HD), lambda l, h: (l, 0, h))
    flat = pl.BlockSpec((1, LEN, 2 * HD), lambda l, h: (l, 0, h))
    terms = pl.BlockSpec((2, 1, PREFIX, HD), lambda l, h: (0, l, 0, h))
    return pl.pallas_call(
        attend_kernel,
        grid=(layers, heads),
        in_specs=[wide, own, own, pre, pre, wide],
        out_specs=[wide, flat, terms],
        out_shape=[
            jax.ShapeDtypeStruct(queries.shape, jnp.bfloat16),
            jax.ShapeDtypeStruct((layers, LEN, 2 * width), jnp.bfloat16),
            jax.ShapeDtypeStruct((2, layers, PREFIX, width), jnp.float32),
        ],
        compiler_params=pltpu.CompilerParams(vmem_limit_bytes=VMEM_LIMIT),
        cost_estimate=COST,
    )(queries, keys, values, prefix_keys, prefix_values, dout)


def project_kernel(y_ref, f0, f1, f2, f3, w0, w1, w2, w3, out_ref):
    total = None
    for f, w in zip((f0, f1, f2, f3), (w0, w1, w2, w3)):
        term = dot(f[0], w[...].reshape(-1, w.shape[-1]), NT)
        total = term if total is None else total + term
    out_ref[0] = total.astype(jnp.bfloat16)


def project(flats, weights, y):
    layers, tokens, depth = flats[0].shape
    rows = weights.shape[4]
    step = 2
    flat_spec = pl.BlockSpec((1, tokens, depth), lambda l, n, y_ref: (l, 0, 0))

    def weight_spec(shift):
        return pl.BlockSpec(
            (1, step, 2, 1, rows, depth),
            lambda l, n, y_ref: (lax.rem(y_ref[0] + 4 - shift, 4), n, 0, l, 0, 0),
        )

    return pl.pallas_call(
        project_kernel,
        grid_spec=pltpu.PrefetchScalarGridSpec(
            num_scalar_prefetch=1,
            grid=(layers, 8 // step),
            in_specs=[flat_spec] * 4 + [weight_spec(s) for s in range(4)],
            out_specs=pl.BlockSpec((1, tokens, step * 2 * rows), lambda l, n, y_ref: (l, 0, n)),
        ),
        out_shape=jax.ShapeDtypeStruct((layers, tokens, 16 * rows), jnp.bfloat16),
        compiler_params=pltpu.CompilerParams(vmem_limit_bytes=VMEM_LIMIT),
        cost_estimate=COST,
    )(y, *flats, weights, weights, weights, weights)


def gate_kernel(*refs):
    pass


def gate(*arrays):
    anywhere = [pl.BlockSpec(memory_space=pl.ANY)] * len(arrays)
    return pl.pallas_call(
        gate_kernel,
        in_specs=anywhere,
        out_specs=anywhere,
        out_shape=[jax.ShapeDtypeStruct(a.shape, a.dtype) for a in arrays],
        input_output_aliases={i: i for i in range(len(arrays))},
        cost_estimate=BRIEF,
    )(*arrays)


def ring(count, shift):
    return [(i, (i + shift) % count) for i in range(count)]


def swap_cores(a):
    return lax.ppermute(a, "core", [(0, 1), (1, 0)])


def turn(a, shift):
    pairs = [(i * 4 + j, (j + shift) % 4 * 4 + i) for i in range(4) for j in range(4)]
    return lax.ppermute(a, ("x", "y"), pairs)


def sum_prefix(terms, core):
    shape = terms.shape[1:]
    keep = jnp.where(core == 0, terms[0], terms[1])
    send = jnp.where(core == 0, terms[1], terms[0])
    half = (keep + swap_cores(send)).reshape(-1, shape[-1])
    half = lax.all_to_all(half, ("x", "z"), 0, 0, tiled=True)
    share = jnp.sum(half.reshape(32, -1, shape[-1]), axis=0, keepdims=True)
    half = jnp.broadcast_to(share, (32,) + share.shape[1:]).reshape(half.shape)
    half = lax.all_to_all(half, ("x", "z"), 0, 0, tiled=True).reshape(shape)
    other = swap_cores(half)
    return jnp.where(core == 0, half, other), jnp.where(core == 0, other, half)


def shards(queries, keys, values, prefix_keys, prefix_values, dout, key_weight, value_weight):
    y = lax.axis_index("y").astype(jnp.int32).reshape(1)
    core = lax.axis_index("core")

    unit = jnp.concatenate(
        [w[:, :, h : h + HD] for h in (0, HD) for w in (key_weight, value_weight)], axis=2
    )
    weights = lax.all_gather(turn(unit, 0), ("x", "z", "core"), axis=0)
    weights = weights.reshape((4, 8, 2) + unit.shape)

    grad_queries, flat, terms = attend_back(
        queries, keys, values, prefix_keys, prefix_values, dout
    )
    flats = [flat] + [lax.ppermute(flat, "y", ring(4, q)) for q in (1, 2, 3)]
    grad_prefix_keys, grad_prefix_values = sum_prefix(terms, core)
    *flats, grad_prefix_keys, grad_prefix_values = gate(
        *flats, grad_prefix_keys, grad_prefix_values
    )
    grad_input = project(flats, weights, y)
    return grad_queries, grad_input, grad_prefix_keys, grad_prefix_values


def solution(mesh):
    mesh = Mesh(mesh.devices.reshape(4, 8, 2, 4), ("x", "z", "core", "y"))
    dp = ("x", "z", "core")
    split = P(None, dp, "y")
    shared = P(None, None, "y")
    in_specs = (split, split, split, shared, shared, split, split, split)
    out_specs = (split, split, shared, shared)
    return jax.shard_map(shards, mesh=mesh, in_specs=in_specs, out_specs=out_specs, check_vma=False)
```

```python
import functools
import math

import jax
import jax.numpy as jnp
from jax import lax
from jax.experimental import pallas as pl
from jax.experimental.pallas import tpu as pltpu
from jax.sharding import Mesh
from jax.sharding import PartitionSpec as P

QH = 64
KVH = 8
HD = 128
LEN = 256
PREFIX = 128
GROUP = QH // KVH
SCALE = HD ** (-0.5)
VMEM_LIMIT = 60 * 1024 * 1024
EXP2 = SCALE * math.log2(math.e)
COST = pl.CostEstimate(flops=2 * 10**9, bytes_accessed=16 * 10**6, transcendentals=0)
BRIEF = pl.CostEstimate(flops=1, bytes_accessed=1, transcendentals=0)

NT = (((1,), (1,)), ((), ()))
NN = (((1,), (0,)), ((), ()))
TN = (((0,), (0,)), ((), ()))


def dot(a, b, dims):
    return lax.dot_general(a, b, dims, preferred_element_type=jnp.float32)


def attend_kernel(q_ref, k_ref, v_ref, pk_ref, pv_ref, do_ref, gq_ref, flat_ref, terms_ref):
    half = LEN // 2
    keys = jnp.concatenate([pk_ref[0], k_ref[0]], axis=0)
    values = jnp.concatenate([pv_ref[0], v_ref[0]], axis=0)
    key_row = lax.broadcasted_iota(jnp.int32, (half, 2 * half), 0)
    token = lax.rem(lax.broadcasted_iota(jnp.int32, (half, 2 * half), 1), half)
    visible = key_row <= token
    key_terms = [0.0, 0.0]
    value_terms = [0.0, 0.0]
    for pair in range(GROUP // 2):
        for part in range(2):
            rows = PREFIX + (part + 1) * half
            tokens = slice(part * half, (part + 1) * half)
            columns = [slice((2 * pair + i) * HD, (2 * pair + i + 1) * HD) for i in range(2)]
            q = jnp.concatenate([q_ref[0, tokens, c] for c in columns], axis=0)
            do = jnp.concatenate([do_ref[0, tokens, c] for c in columns], axis=0)
            scores = dot(keys[:rows], q, NT)
            last = jnp.where(visible, scores[rows - half :], -1e30)
            scores = jnp.concatenate([scores[: rows - half], last], axis=0)
            peak = jnp.max(scores, axis=0, keepdims=True)
            exp_scores = jnp.exp2((scores - peak) * EXP2)
            probs = exp_scores * (1.0 / jnp.sum(exp_scores, axis=0, keepdims=True))
            dprobs = dot(values[:rows], do, NT)
            row_delta = jnp.sum(probs * dprobs, axis=0, keepdims=True)
            dscores = (probs * (dprobs - row_delta)).astype(jnp.bfloat16)
            gq = (dot(dscores, keys[:rows], TN) * SCALE).astype(jnp.bfloat16)
            for i, c in enumerate(columns):
                gq_ref[0, tokens, c] = gq[i * half : (i + 1) * half]
            key_terms[part] += dot(dscores, q, NN)
            value_terms[part] += dot(probs.astype(jnp.bfloat16), do, NN)
    split = PREFIX + half
    for i, (terms, scale) in enumerate(((key_terms, SCALE), (value_terms, 1.0))):
        low = (terms[0] + terms[1][:split]) * scale
        high = terms[1][split:] * scale
        flat_ref[0, :half, i * HD : (i + 1) * HD] = low[PREFIX:].astype(jnp.bfloat16)
        flat_ref[0, half:, i * HD : (i + 1) * HD] = high.astype(jnp.bfloat16)
        terms_ref[i, 0, 0] = low[:PREFIX]


def attend_back(queries, keys, values, prefix_keys, prefix_values, dout):
    layers, _, width = keys.shape
    heads = width // HD
    wide = pl.BlockSpec((1, LEN, GROUP * HD), lambda l, h: (l, 0, h))
    own = pl.BlockSpec((1, LEN, HD), lambda l, h: (l, 0, h))
    pre = pl.BlockSpec((1, PREFIX, HD), lambda l, h: (l, 0, h))
    flat = pl.BlockSpec((1, LEN, 2 * HD), lambda l, h: (l, 0, h))
    terms = pl.BlockSpec((2, 1, 1, PREFIX, HD), lambda l, h: (0, l, h, 0, 0))
    return pl.pallas_call(
        attend_kernel,
        grid=(layers, heads),
        in_specs=[wide, own, own, pre, pre, wide],
        out_specs=[wide, flat, terms],
        out_shape=[
            jax.ShapeDtypeStruct(queries.shape, jnp.bfloat16),
            jax.ShapeDtypeStruct((layers, LEN, 2 * width), jnp.bfloat16),
            jax.ShapeDtypeStruct((2, layers, heads, PREFIX, HD), jnp.float32),
        ],
        compiler_params=pltpu.CompilerParams(vmem_limit_bytes=VMEM_LIMIT),
        cost_estimate=COST,
    )(queries, keys, values, prefix_keys, prefix_values, dout)


def project_kernel(y_ref, f0, f1, f2, f3, w0, w1, w2, w3, out_ref):
    total = None
    for f, w in zip((f0, f1, f2, f3), (w0, w1, w2, w3)):
        term = dot(f[0], w[...].reshape(-1, w.shape[-1]), NT)
        total = term if total is None else total + term
    out_ref[0] = total.astype(jnp.bfloat16)


def project(flats, weights, y):
    layers, tokens, depth = flats[0].shape
    rows = weights.shape[4]
    step = 4
    flat_spec = pl.BlockSpec((1, tokens, depth), lambda l, n, y_ref: (l, 0, 0))

    def weight_spec(shift):
        return pl.BlockSpec(
            (1, step, 2, 1, rows, depth),
            lambda l, n, y_ref: (lax.rem(y_ref[0] + 4 - shift + 2 * l, 4), n, 0, l, 0, 0),
        )

    return pl.pallas_call(
        project_kernel,
        grid_spec=pltpu.PrefetchScalarGridSpec(
            num_scalar_prefetch=1,
            grid=(layers, 8 // step),
            in_specs=[flat_spec] * 4 + [weight_spec(s) for s in range(4)],
            out_specs=pl.BlockSpec((1, tokens, step * 2 * rows), lambda l, n, y_ref: (l, 0, n)),
        ),
        out_shape=jax.ShapeDtypeStruct((layers, tokens, 16 * rows), jnp.bfloat16),
        compiler_params=pltpu.CompilerParams(vmem_limit_bytes=VMEM_LIMIT),
        cost_estimate=COST,
    )(y, *flats, weights, weights, weights, weights)


def gate_kernel(*refs):
    pass


def gate(*arrays):
    anywhere = [pl.BlockSpec(memory_space=pl.ANY)] * len(arrays)
    return pl.pallas_call(
        gate_kernel,
        in_specs=anywhere,
        out_specs=anywhere,
        out_shape=[jax.ShapeDtypeStruct(a.shape, a.dtype) for a in arrays],
        input_output_aliases={i: i for i in range(len(arrays))},
        cost_estimate=BRIEF,
    )(*arrays)


def ring(count, shift):
    return [(i, (i + shift) % count) for i in range(count)]


def swap_cores(a):
    return lax.ppermute(a, "core", [(0, 1), (1, 0)])


def turn(a, shift):
    pairs = [(i * 4 + j, (j + shift) % 4 * 4 + i) for i in range(4) for j in range(4)]
    return lax.ppermute(a, ("x", "y"), pairs)


def exchange(a):
    return lax.all_to_all(a, ("x", "z"), 0, 0, tiled=True)


def sum_prefix(terms, core):
    keep = jnp.where(core == 0, terms[0], terms[1])
    send = jnp.where(core == 0, terms[1], terms[0])
    share = exchange((keep + swap_cores(send)).astype(jnp.bfloat16).reshape(-1, HD))
    share = jnp.sum(share.reshape(32, -1, HD).astype(jnp.float32), axis=0, keepdims=True)
    share = jnp.broadcast_to(share.astype(jnp.bfloat16), (32,) + share.shape[1:])
    share = exchange(share.reshape(-1, HD))
    other = swap_cores(share)

    def whole(a, b):
        a = jnp.where(core == 0, a, b).reshape(terms.shape[1:]).transpose(0, 2, 1, 3)
        return a.astype(jnp.float32).reshape(2, PREFIX, -1)

    return whole(share, other), whole(other, share)


def shards(queries, keys, values, prefix_keys, prefix_values, dout, key_weight, value_weight):
    y = lax.axis_index("y").astype(jnp.int32).reshape(1)
    core = lax.axis_index("core")

    unit = jnp.concatenate(
        [w[:, :, h : h + HD] for h in (0, HD) for w in (key_weight, value_weight)], axis=2
    )
    turned = jnp.stack([turn(unit[0], 0), turn(unit[1], 2)])
    weights = lax.all_gather(turned, ("x", "z", "core"), axis=0)
    weights = weights.reshape((4, 8, 2) + unit.shape)

    grad_queries, flat, terms = attend_back(
        queries, keys, values, prefix_keys, prefix_values, dout
    )
    flats = [flat] + [lax.ppermute(flat, "y", ring(4, q)) for q in (1, 2, 3)]
    grad_prefix_keys, grad_prefix_values = sum_prefix(terms, core)
    *flats, grad_prefix_keys, grad_prefix_values = gate(
        *flats, grad_prefix_keys, grad_prefix_values
    )
    grad_input = project(flats, weights, y)
    return grad_queries, grad_input, grad_prefix_keys, grad_prefix_values


def solution(mesh):
    mesh = Mesh(mesh.devices.reshape(4, 8, 2, 4), ("x", "z", "core", "y"))
    dp = ("x", "z", "core")
    split = P(None, dp, "y")
    shared = P(None, None, "y")
    in_specs = (split, split, split, shared, shared, split, split, split)
    out_specs = (split, split, shared, shared)
    return jax.shard_map(shards, mesh=mesh, in_specs=in_specs, out_specs=out_specs, check_vma=False)
```

```python
import functools
import math

import jax
import jax.numpy as jnp
from jax import lax
from jax.experimental import pallas as pl
from jax.experimental.pallas import tpu as pltpu
from jax.sharding import Mesh
from jax.sharding import PartitionSpec as P

QH = 64
KVH = 8
HD = 128
LEN = 256
PREFIX = 128
GROUP = QH // KVH
SCALE = HD ** (-0.5)
VMEM_LIMIT = 60 * 1024 * 1024
EXP2 = SCALE * math.log2(math.e)
COST = pl.CostEstimate(flops=2 * 10**9, bytes_accessed=16 * 10**6, transcendentals=0)
BRIEF = pl.CostEstimate(flops=1, bytes_accessed=1, transcendentals=0)

NT = (((1,), (1,)), ((), ()))
NN = (((1,), (0,)), ((), ()))
TN = (((0,), (0,)), ((), ()))


def dot(a, b, dims):
    return lax.dot_general(a, b, dims, preferred_element_type=jnp.float32)


def attend_kernel(q_ref, k_ref, v_ref, pk_ref, pv_ref, do_ref, gq_ref, flat_ref, terms_ref):
    half = LEN // 2
    keys = jnp.concatenate([pk_ref[0], k_ref[0]], axis=0)
    values = jnp.concatenate([pv_ref[0], v_ref[0]], axis=0)
    key_row = lax.broadcasted_iota(jnp.int32, (half, 2 * half), 0)
    token = lax.rem(lax.broadcasted_iota(jnp.int32, (half, 2 * half), 1), half)
    visible = key_row <= token
    key_terms = [0.0, 0.0]
    value_terms = [0.0, 0.0]
    for pair in range(GROUP // 2):
        for part in range(2):
            rows = PREFIX + (part + 1) * half
            tokens = slice(part * half, (part + 1) * half)
            columns = [slice((2 * pair + i) * HD, (2 * pair + i + 1) * HD) for i in range(2)]
            q = jnp.concatenate([q_ref[0, tokens, c] for c in columns], axis=0)
            do = jnp.concatenate([do_ref[0, tokens, c] for c in columns], axis=0)
            scores = dot(keys[:rows], q, NT)
            last = jnp.where(visible, scores[rows - half :], -1e30)
            scores = jnp.concatenate([scores[: rows - half], last], axis=0)
            peak = jnp.max(scores, axis=0, keepdims=True)
            exp_scores = jnp.exp2((scores - peak) * EXP2)
            probs = exp_scores * (1.0 / jnp.sum(exp_scores, axis=0, keepdims=True))
            dprobs = dot(values[:rows], do, NT)
            row_delta = jnp.sum(probs * dprobs, axis=0, keepdims=True)
            dscores = (probs * (dprobs - row_delta)).astype(jnp.bfloat16)
            gq = (dot(dscores, keys[:rows], TN) * SCALE).astype(jnp.bfloat16)
            for i, c in enumerate(columns):
                gq_ref[0, tokens, c] = gq[i * half : (i + 1) * half]
            key_terms[part] += dot(dscores, q, NN)
            value_terms[part] += dot(probs.astype(jnp.bfloat16), do, NN)
    split = PREFIX + half
    for i, (terms, scale) in enumerate(((key_terms, SCALE), (value_terms, 1.0))):
        low = (terms[0] + terms[1][:split]) * scale
        high = terms[1][split:] * scale
        columns = pl.ds(pl.multiple_of((2 * i + pl.program_id(1)) * HD, HD), HD)
        flat_ref[0, :half, columns] = low[PREFIX:].astype(jnp.bfloat16)
        flat_ref[0, half:, columns] = high.astype(jnp.bfloat16)
        terms_ref[i, 0, 0] = low[:PREFIX]


def attend_back(queries, keys, values, prefix_keys, prefix_values, dout):
    layers, _, width = keys.shape
    heads = width // HD
    wide = pl.BlockSpec((1, LEN, GROUP * HD), lambda l, h: (l, 0, h))
    own = pl.BlockSpec((1, LEN, HD), lambda l, h: (l, 0, h))
    pre = pl.BlockSpec((1, PREFIX, HD), lambda l, h: (l, 0, h))
    flat = pl.BlockSpec((1, LEN, 2 * width), lambda l, h: (l, 0, 0))
    terms = pl.BlockSpec((2, 1, 1, PREFIX, HD), lambda l, h: (0, l, h, 0, 0))
    return pl.pallas_call(
        attend_kernel,
        grid=(layers, heads),
        in_specs=[wide, own, own, pre, pre, wide],
        out_specs=[wide, flat, terms],
        out_shape=[
            jax.ShapeDtypeStruct(queries.shape, jnp.bfloat16),
            jax.ShapeDtypeStruct((layers, LEN, 2 * width), jnp.bfloat16),
            jax.ShapeDtypeStruct((2, layers, heads, PREFIX, HD), jnp.float32),
        ],
        compiler_params=pltpu.CompilerParams(vmem_limit_bytes=VMEM_LIMIT),
        cost_estimate=COST,
    )(queries, keys, values, prefix_keys, prefix_values, dout)


def project_kernel(y_ref, f0, f1, f2, f3, *refs):
    flats, weight_refs, out_ref = (f0, f1, f2, f3), refs[:-1], refs[-1]
    total = None
    for s in range(4):
        even, odd = weight_refs[2 * s], weight_refs[2 * s + 1]
        rows = [w[0, n, 0, 0] for n in range(even.shape[1]) for w in (even, odd)]
        term = dot(flats[s][0], jnp.concatenate(rows, axis=0), NT)
        total = term if total is None else total + term
    out_ref[0] = total.astype(jnp.bfloat16)


def project(flats, weights, y):
    layers, tokens, depth = flats[0].shape
    rows = weights.shape[4]
    step = 4
    flat_spec = pl.BlockSpec((1, tokens, depth), lambda l, n, y_ref: (l, 0, 0))

    def weight_spec(s, core):
        return pl.BlockSpec(
            (1, step, 1, 1, rows, depth),
            lambda l, n, y_ref: (lax.rem(y_ref[0] + 4 - s + 2 * core, 4), n, core, l, 0, 0),
        )

    return pl.pallas_call(
        project_kernel,
        grid_spec=pltpu.PrefetchScalarGridSpec(
            num_scalar_prefetch=1,
            grid=(layers, 8 // step),
            in_specs=[flat_spec] * 4 + [weight_spec(s, core) for s in range(4) for core in range(2)],
            out_specs=pl.BlockSpec((1, tokens, step * 2 * rows), lambda l, n, y_ref: (l, 0, n)),
        ),
        out_shape=jax.ShapeDtypeStruct((layers, tokens, 16 * rows), jnp.bfloat16),
        compiler_params=pltpu.CompilerParams(vmem_limit_bytes=VMEM_LIMIT),
        cost_estimate=COST,
    )(y, *flats, *[weights] * 8)


def gate_kernel(*refs):
    pass


def gate(*arrays):
    anywhere = [pl.BlockSpec(memory_space=pl.ANY)] * len(arrays)
    return pl.pallas_call(
        gate_kernel,
        in_specs=anywhere,
        out_specs=anywhere,
        out_shape=[jax.ShapeDtypeStruct(a.shape, a.dtype) for a in arrays],
        input_output_aliases={i: i for i in range(len(arrays))},
        cost_estimate=BRIEF,
    )(*arrays)


def ring(count, shift):
    return [(i, (i + shift) % count) for i in range(count)]


def swap_cores(a):
    return lax.ppermute(a, "core", [(0, 1), (1, 0)])


def turn(a, shift):
    pairs = []
    for x in range(4):
        for core in range(2):
            for y in range(4):
                there = ((y + 2 * core + shift) % 4 * 2 + core) * 4 + x
                pairs.append(((x * 2 + core) * 4 + y, there))
    return lax.ppermute(a, ("x", "core", "y"), pairs)


def exchange(a):
    return lax.all_to_all(a, ("x", "z"), 0, 0, tiled=True)


def sum_prefix(terms, core):
    keep = jnp.where(core == 0, terms[0], terms[1])
    send = jnp.where(core == 0, terms[1], terms[0])
    share = exchange((keep + swap_cores(send)).astype(jnp.bfloat16).reshape(-1, HD))
    share = jnp.sum(share.reshape(32, -1, HD).astype(jnp.float32), axis=0, keepdims=True)
    share = jnp.broadcast_to(share.astype(jnp.bfloat16), (32,) + share.shape[1:])
    share = exchange(share.reshape(-1, HD))
    other = swap_cores(share)

    def whole(a, b):
        a = jnp.where(core == 0, a, b).reshape(terms.shape[1:]).transpose(0, 2, 1, 3)
        return a.astype(jnp.float32).reshape(2, PREFIX, -1)

    return whole(share, other), whole(other, share)


def shards(queries, keys, values, prefix_keys, prefix_values, dout, key_weight, value_weight):
    y = lax.axis_index("y").astype(jnp.int32).reshape(1)
    core = lax.axis_index("core")

    turned = turn(jnp.concatenate([key_weight, value_weight], axis=2), 0)
    weights = lax.all_gather(turned, ("x", "z", "core"), axis=0)
    weights = weights.reshape((4, 8, 2) + turned.shape)

    grad_queries, flat, terms = attend_back(
        queries, keys, values, prefix_keys, prefix_values, dout
    )
    flats = [flat] + [lax.ppermute(flat, "y", ring(4, q)) for q in (1, 2, 3)]
    grad_prefix_keys, grad_prefix_values = sum_prefix(terms, core)
    *flats, grad_prefix_keys, grad_prefix_values = gate(
        *flats, grad_prefix_keys, grad_prefix_values
    )
    grad_input = project(flats, weights, y)
    return grad_queries, grad_input, grad_prefix_keys, grad_prefix_values


def solution(mesh):
    mesh = Mesh(mesh.devices.reshape(4, 8, 2, 4), ("x", "z", "core", "y"))
    dp = ("x", "z", "core")
    split = P(None, dp, "y")
    shared = P(None, None, "y")
    in_specs = (split, split, split, shared, shared, split, split, split)
    out_specs = (split, split, shared, shared)
    return jax.shard_map(shards, mesh=mesh, in_specs=in_specs, out_specs=out_specs, check_vma=False)
```

```python
import functools
import math

import jax
import jax.numpy as jnp
from jax import lax
from jax.experimental import pallas as pl
from jax.experimental.pallas import tpu as pltpu
from jax.sharding import Mesh
from jax.sharding import PartitionSpec as P

QH = 64
KVH = 8
HD = 128
LEN = 256
PREFIX = 128
GROUP = QH // KVH
SCALE = HD ** (-0.5)
VMEM_LIMIT = 60 * 1024 * 1024
EXP2 = SCALE * math.log2(math.e)
COST = pl.CostEstimate(flops=2 * 10**9, bytes_accessed=16 * 10**6, transcendentals=0)
BRIEF = pl.CostEstimate(flops=1, bytes_accessed=1, transcendentals=0)

NT = (((1,), (1,)), ((), ()))
NN = (((1,), (0,)), ((), ()))
TN = (((0,), (0,)), ((), ()))


def dot(a, b, dims):
    return lax.dot_general(a, b, dims, preferred_element_type=jnp.float32)


def attend_kernel(q_ref, k_ref, v_ref, pk_ref, pv_ref, do_ref, gq_ref, flat_ref, terms_ref):
    half = LEN // 2
    keys = jnp.concatenate([pk_ref[0], k_ref[0]], axis=0)
    values = jnp.concatenate([pv_ref[0], v_ref[0]], axis=0)
    key_row = lax.broadcasted_iota(jnp.int32, (half, 2 * half), 0)
    token = lax.rem(lax.broadcasted_iota(jnp.int32, (half, 2 * half), 1), half)
    visible = key_row <= token
    key_terms = [0.0, 0.0]
    value_terms = [0.0, 0.0]
    for pair in range(GROUP // 2):
        for part in range(2):
            rows = PREFIX + (part + 1) * half
            tokens = slice(part * half, (part + 1) * half)
            columns = [slice((2 * pair + i) * HD, (2 * pair + i + 1) * HD) for i in range(2)]
            q = jnp.concatenate([q_ref[0, tokens, c] for c in columns], axis=0)
            do = jnp.concatenate([do_ref[0, tokens, c] for c in columns], axis=0)
            scores = dot(keys[:rows], q, NT)
            last = jnp.where(visible, scores[rows - half :], -1e30)
            scores = jnp.concatenate([scores[: rows - half], last], axis=0)
            peak = jnp.max(scores, axis=0, keepdims=True)
            exp_scores = jnp.exp2((scores - peak) * EXP2)
            probs = exp_scores * (1.0 / jnp.sum(exp_scores, axis=0, keepdims=True))
            dprobs = dot(values[:rows], do, NT)
            row_delta = jnp.sum(probs * dprobs, axis=0, keepdims=True)
            dscores = (probs * (dprobs - row_delta)).astype(jnp.bfloat16)
            gq = (dot(dscores, keys[:rows], TN) * SCALE).astype(jnp.bfloat16)
            for i, c in enumerate(columns):
                gq_ref[0, tokens, c] = gq[i * half : (i + 1) * half]
            key_terms[part] += dot(dscores, q, NN)
            value_terms[part] += dot(probs.astype(jnp.bfloat16), do, NN)
    split = PREFIX + half
    for i, (terms, scale) in enumerate(((key_terms, SCALE), (value_terms, 1.0))):
        low = (terms[0] + terms[1][:split]) * scale
        high = terms[1][split:] * scale
        columns = pl.ds(pl.multiple_of((2 * i + pl.program_id(1)) * HD, HD), HD)
        flat_ref[0, :half, columns] = low[PREFIX:].astype(jnp.bfloat16)
        flat_ref[0, half:, columns] = high.astype(jnp.bfloat16)
        terms_ref[i, 0, 0] = low[:PREFIX]


def attend_back(queries, keys, values, prefix_keys, prefix_values, dout):
    layers, _, width = keys.shape
    heads = width // HD
    wide = pl.BlockSpec((1, LEN, GROUP * HD), lambda l, h: (l, 0, h))
    own = pl.BlockSpec((1, LEN, HD), lambda l, h: (l, 0, h))
    pre = pl.BlockSpec((1, PREFIX, HD), lambda l, h: (l, 0, h))
    flat = pl.BlockSpec((1, LEN, 2 * width), lambda l, h: (l, 0, 0))
    terms = pl.BlockSpec((2, 1, 1, PREFIX, HD), lambda l, h: (0, l, h, 0, 0))
    return pl.pallas_call(
        attend_kernel,
        grid=(layers, heads),
        in_specs=[wide, own, own, pre, pre, wide],
        out_specs=[wide, flat, terms],
        out_shape=[
            jax.ShapeDtypeStruct(queries.shape, jnp.bfloat16),
            jax.ShapeDtypeStruct((layers, LEN, 2 * width), jnp.bfloat16),
            jax.ShapeDtypeStruct((2, layers, heads, PREFIX, HD), jnp.float32),
        ],
        compiler_params=pltpu.CompilerParams(vmem_limit_bytes=VMEM_LIMIT),
        cost_estimate=COST,
    )(queries, keys, values, prefix_keys, prefix_values, dout)


def project_kernel(y_ref, f0, f1, f2, f3, *refs):
    flats, weight_refs, out_ref = (f0, f1, f2, f3), refs[:-1], refs[-1]
    total = None
    for s in range(4):
        even, odd = weight_refs[2 * s], weight_refs[2 * s + 1]
        rows = [w[0, n, 0, 0] for n in range(even.shape[1]) for w in (even, odd)]
        term = dot(flats[s][0], jnp.concatenate(rows, axis=0), NT)
        total = term if total is None else total + term
    out_ref[0] = total.astype(jnp.bfloat16)


def project(flats, weights, y):
    layers, tokens, depth = flats[0].shape
    rows = weights.shape[4]
    step = 8
    flat_spec = pl.BlockSpec((1, tokens, depth), lambda l, n, y_ref: (l, 0, 0))

    def weight_spec(s, core):
        return pl.BlockSpec(
            (1, step, 1, 1, rows, depth),
            lambda l, n, y_ref: (lax.rem(y_ref[0] + 4 - s + 2 * core, 4), n, core, l, 0, 0),
        )

    return pl.pallas_call(
        project_kernel,
        grid_spec=pltpu.PrefetchScalarGridSpec(
            num_scalar_prefetch=1,
            grid=(layers, 8 // step),
            in_specs=[flat_spec] * 4 + [weight_spec(s, core) for s in range(4) for core in range(2)],
            out_specs=pl.BlockSpec((1, tokens, step * 2 * rows), lambda l, n, y_ref: (l, 0, n)),
        ),
        out_shape=jax.ShapeDtypeStruct((layers, tokens, 16 * rows), jnp.bfloat16),
        compiler_params=pltpu.CompilerParams(vmem_limit_bytes=VMEM_LIMIT),
        cost_estimate=COST,
    )(y, *flats, *[weights] * 8)


def gate_kernel(*refs):
    pass


def gate(*arrays):
    anywhere = [pl.BlockSpec(memory_space=pl.ANY)] * len(arrays)
    return pl.pallas_call(
        gate_kernel,
        in_specs=anywhere,
        out_specs=anywhere,
        out_shape=[jax.ShapeDtypeStruct(a.shape, a.dtype) for a in arrays],
        input_output_aliases={i: i for i in range(len(arrays))},
        cost_estimate=BRIEF,
    )(*arrays)


def ring(count, shift):
    return [(i, (i + shift) % count) for i in range(count)]


def swap_cores(a):
    return lax.ppermute(a, "core", [(0, 1), (1, 0)])


def turn(a, shift):
    pairs = []
    for x in range(4):
        for core in range(2):
            for y in range(4):
                there = ((y + 2 * core + shift) % 4 * 2 + core) * 4 + x
                pairs.append(((x * 2 + core) * 4 + y, there))
    return lax.ppermute(a, ("x", "core", "y"), pairs)


def exchange(a):
    return lax.all_to_all(a, ("x", "z"), 0, 0, tiled=True)


def sum_prefix(terms, core):
    keep = jnp.where(core == 0, terms[0], terms[1])
    send = jnp.where(core == 0, terms[1], terms[0])
    share = exchange((keep + swap_cores(send)).astype(jnp.bfloat16).reshape(-1, HD))
    share = jnp.sum(share.reshape(32, -1, HD).astype(jnp.float32), axis=0, keepdims=True)
    share = jnp.broadcast_to(share.astype(jnp.bfloat16), (32,) + share.shape[1:])
    share = exchange(share.reshape(-1, HD))
    other = swap_cores(share)

    def whole(a, b):
        a = jnp.where(core == 0, a, b).reshape(terms.shape[1:]).transpose(0, 2, 1, 3)
        return a.astype(jnp.float32).reshape(2, PREFIX, -1)

    return whole(share, other), whole(other, share)


def shards(queries, keys, values, prefix_keys, prefix_values, dout, key_weight, value_weight):
    y = lax.axis_index("y").astype(jnp.int32).reshape(1)
    core = lax.axis_index("core")

    turned = turn(jnp.concatenate([key_weight, value_weight], axis=2), 0)
    weights = lax.all_gather(turned, ("x", "z", "core"), axis=0)
    weights = weights.reshape((4, 8, 2) + turned.shape)

    grad_queries, flat, terms = attend_back(
        queries, keys, values, prefix_keys, prefix_values, dout
    )
    flats = [flat] + [lax.ppermute(flat, "y", ring(4, q)) for q in (1, 2, 3)]
    grad_prefix_keys, grad_prefix_values = sum_prefix(terms, core)
    *flats, grad_prefix_keys, grad_prefix_values = gate(
        *flats, grad_prefix_keys, grad_prefix_values
    )
    grad_input = project(flats, weights, y)
    return grad_queries, grad_input, grad_prefix_keys, grad_prefix_values


def solution(mesh):
    mesh = Mesh(mesh.devices.reshape(4, 8, 2, 4), ("x", "z", "core", "y"))
    dp = ("x", "z", "core")
    split = P(None, dp, "y")
    shared = P(None, None, "y")
    in_specs = (split, split, split, shared, shared, split, split, split)
    out_specs = (split, split, shared, shared)
    return jax.shard_map(shards, mesh=mesh, in_specs=in_specs, out_specs=out_specs, check_vma=False)
```
